32 devices in a mesh: grp: 1, row: 32 (over z, y, x, core).
Axes of the slice: x: 2, y: 2, z: 4, core: 2. Of those that a mesh axis runs over, the one named last changes fastest.
Arguments:
- pair_map: bfloat16 [128, 128, 128], P(('grp', 'row')), may hold values from -6 to 6
- single: bfloat16 [128, 384], P(('grp', 'row')), may hold values from -6 to 6
- noise_term: bfloat16 [128, 384], P(('grp', 'row')), may hold values from -3 to 3
- token_mask: int32 [128], P('grp'), may hold values 0 or 1
- w_mul_in: bfloat16 [128, 512], replicated, may hold values from -0.5 to 0.5
- w_mul_gate: bfloat16 [128, 128], replicated, may hold values from -0.5 to 0.5
- w_mul_out: bfloat16 [128, 128], replicated, may hold values from -0.5 to 0.5
- w_att_in: bfloat16 [128, 512], replicated, may hold values from -0.5 to 0.5
- w_att_bias: bfloat16 [128, 4], replicated, may hold values from -0.5 to 0.5
- w_att_out: bfloat16 [128, 128], replicated, may hold values from -0.5 to 0.5
- w_tok_in: bfloat16 [384, 1536], replicated, may hold values from -0.3125 to 0.3125
- w_pair_bias: bfloat16 [128, 16], replicated, may hold values from -0.5 to 0.5
- w_tok_out: bfloat16 [384, 384], replicated, may hold values from -0.3125 to 0.3125
Outputs:
- pair_out: bfloat16 [128, 128, 128], P(('grp', 'row'))
- token_out: bfloat16 [128, 384], P(('grp', 'row'))
The draws below stay inside these ranges and needn't reach their ends.
All inputs are finite; a program needn't handle non-finite values.
Results may differ from the reference program's by a relative error of at most 0.0085.
Values may be sent and summed in bfloat16 or wider, within the bound.
A program may use at most 64 MiB of HBM per device.

```python
import jax
import jax.numpy as jnp
from jax import lax

PAIR_C = 128
MUL_C = 128
SINGLE_C = 384
TRI_HEADS = 4
TOK_HEADS = 16
TOKENS = 128


def touch_ends(drawn, key, smallest, largest):
    extent = drawn.shape
    place = [jax.random.randint(jax.random.fold_in(key, axis), (), 0, extent[axis]) for axis in range(len(extent))]
    drawn = drawn.at[tuple(place)].set(smallest)
    longest = extent.index(max(extent))
    place[longest] = (place[longest] + 1) % extent[longest]
    return drawn.at[tuple(place)].set(largest)


def level_of(key, shape, cuts, least, largest):
    factor_of = 1.0
    for position, parts in cuts:
        steps = jax.random.uniform(jax.random.fold_in(jax.random.fold_in(key, 6), position), (parts,), jnp.float32, least / len(cuts), largest / len(cuts))
        factor_of = factor_of * jnp.repeat(jnp.exp(steps), shape[position] // parts).reshape((-1,) + (1,) * (len(shape) - 1 - position))
    return factor_of


def normal_values(own_key, dims, scale, bound, pieces=(), held_as=jnp.bfloat16):
    loudness = level_of(own_key, dims, pieces, -0.22, 0.18) if pieces else 1.0
    array = jax.random.normal(own_key, dims, jnp.float32) * scale * loudness
    return jnp.minimum(jnp.maximum(array, -bound), bound).astype(held_as)


def setup_inputs(seed: int = 0, part: int = 0) -> dict:
    keys = jax.random.split(jax.random.key(seed), 14)
    part_keys = jax.random.split(jax.random.fold_in(keys[13], part), 14)
    return {
        "pair_map": normal_values(part_keys[0], (TOKENS, TOKENS, PAIR_C), 1.0, 6.0, ((0, 32),)),
        "single": normal_values(part_keys[1], (TOKENS, SINGLE_C), 1.0, 6.0, ((0, 32),)),
        "noise_term": normal_values(part_keys[2], (TOKENS, SINGLE_C), 0.5, 3.0, ((0, 32),)),
        "token_mask": touch_ends((jax.random.randint(part_keys[3], (TOKENS,), 0, 8) < 7).astype(jnp.int32), jax.random.fold_in(part_keys[3], 1), 0, 1),
        "w_mul_in": normal_values(keys[4], (PAIR_C, 4 * MUL_C), PAIR_C ** -0.5, 0.5),
        "w_mul_gate": normal_values(keys[5], (PAIR_C, PAIR_C), PAIR_C ** -0.5, 0.5),
        "w_mul_out": normal_values(keys[6], (MUL_C, PAIR_C), MUL_C ** -0.5, 0.5),
        "w_att_in": normal_values(keys[7], (PAIR_C, 4 * PAIR_C), PAIR_C ** -0.5, 0.5),
        "w_att_bias": normal_values(keys[8], (PAIR_C, TRI_HEADS), PAIR_C ** -0.5, 0.5),
        "w_att_out": normal_values(keys[9], (PAIR_C, PAIR_C), PAIR_C ** -0.5, 0.5),
        "w_tok_in": normal_values(keys[10], (SINGLE_C, 4 * SINGLE_C), SINGLE_C ** -0.5, 0.3125),
        "w_pair_bias": normal_values(keys[11], (PAIR_C, TOK_HEADS), PAIR_C ** -0.5, 0.5),
        "w_tok_out": normal_values(keys[12], (SINGLE_C, SINGLE_C), SINGLE_C ** -0.5, 0.3125),
    }


def layer_norm(values, along_axis):
    average = lax.optimization_barrier(jnp.mean(values, axis=along_axis, keepdims=True))
    centred = values - average
    spread = lax.optimization_barrier(jnp.mean(centred * centred, axis=along_axis, keepdims=True))
    return centred * lax.rsqrt(spread + 1e-05)

def split_heads(values, head_count):
    return values.reshape(values.shape[:-1] + (head_count, values.shape[-1] // head_count))

def row_attention(query_rows, key_rows, value_rows, bias_block, key_shift, score_scale):
    scores = jnp.einsum('jhd,khd->hjk', query_rows.astype(jnp.float32), key_rows.astype(jnp.float32)) * score_scale
    scores = scores + bias_block.astype(jnp.float32) + key_shift
    weights = jax.nn.softmax(scores, axis=-1).astype(jnp.bfloat16)
    combined = jnp.einsum('hjk,khd->jhd', weights.astype(jnp.float32), value_rows.astype(jnp.float32))
    return combined.reshape(combined.shape[0], -1)

def reference(pair_map, single, noise_term, token_mask, w_mul_in, w_mul_gate, w_mul_out, w_att_in, w_att_bias, w_att_out, w_tok_in, w_pair_bias, w_tok_out):
    f32 = jnp.float32
    bf16 = jnp.bfloat16
    mask_float = token_mask.astype(f32)
    key_shift = jnp.where(token_mask > 0, 0.0, -1000000000.0).astype(f32)
    pair_float = pair_map.astype(f32)
    normed = layer_norm(pair_float, -1).astype(bf16)
    hidden_count = MUL_C
    mixed = jnp.einsum('ijc,cd->dij', normed.astype(f32), w_mul_in.astype(f32))
    pair_mask = mask_float[:, None] * mask_float[None, :]
    left_side = (jax.nn.sigmoid(mixed[:hidden_count]) * mixed[hidden_count:2 * hidden_count] * pair_mask).astype(bf16)
    right_side = (jax.nn.sigmoid(mixed[2 * hidden_count:3 * hidden_count]) * mixed[3 * hidden_count:] * pair_mask).astype(bf16)

    def channel_product(side_pair):
        return jnp.dot(side_pair[0], side_pair[1].T, preferred_element_type=f32).astype(bf16)
    crossed = lax.map(channel_product, (left_side, right_side))
    crossed_norm = layer_norm(crossed.astype(f32), 0).astype(bf16)
    update = jnp.einsum('cij,cd->ijd', crossed_norm.astype(f32), w_mul_out.astype(f32))
    gating = jax.nn.sigmoid(jnp.einsum('ijc,cd->ijd', normed.astype(f32), w_mul_gate.astype(f32)))
    pair_one = (pair_float + gating * update).astype(bf16)
    normed_one = layer_norm(pair_one.astype(f32), -1).astype(bf16)
    projected = jnp.einsum('ijc,cd->ijd', normed_one.astype(f32), w_att_in.astype(f32))
    channels = PAIR_C
    queries = split_heads(projected[..., :channels].astype(bf16), TRI_HEADS)
    keys_in = split_heads(projected[..., channels:2 * channels].astype(bf16), TRI_HEADS)
    values_in = split_heads(projected[..., 2 * channels:3 * channels].astype(bf16), TRI_HEADS)
    gating_att = jax.nn.sigmoid(projected[..., 3 * channels:])
    tri_bias = jnp.einsum('ijc,ch->hij', normed_one.astype(f32), w_att_bias.astype(f32)).astype(bf16)
    tri_scale = (PAIR_C // TRI_HEADS) ** (-0.5)

    def attend_row(row_parts):
        return row_attention(row_parts[0], row_parts[1], row_parts[2], tri_bias, key_shift, tri_scale)
    attended = lax.map(attend_row, (queries, keys_in, values_in))
    attended_gated = (gating_att * attended).astype(bf16)
    pair_out = (pair_one.astype(f32) + jnp.einsum('ijc,cd->ijd', attended_gated.astype(f32), w_att_out.astype(f32))).astype(bf16)
    activity = single.astype(f32) + noise_term.astype(f32)
    token_norm = layer_norm(activity, -1).astype(bf16)
    tok_projected = jnp.dot(token_norm, w_tok_in, preferred_element_type=f32)
    width_tok = SINGLE_C
    tok_queries = split_heads(tok_projected[:, :width_tok].astype(bf16), TOK_HEADS)
    tok_keys = split_heads(tok_projected[:, width_tok:2 * width_tok].astype(bf16), TOK_HEADS)
    tok_values = split_heads(tok_projected[:, 2 * width_tok:3 * width_tok].astype(bf16), TOK_HEADS)
    tok_gate = jax.nn.sigmoid(tok_projected[:, 3 * width_tok:])
    pair_norm = layer_norm(pair_out.astype(f32), -1).astype(bf16)
    pair_bias = jnp.einsum('ijc,ch->hij', pair_norm.astype(f32), w_pair_bias.astype(f32)).astype(bf16)
    tok_scale = (SINGLE_C // TOK_HEADS) ** (-0.5)
    tok_combined = row_attention(tok_queries, tok_keys, tok_values, pair_bias, key_shift, tok_scale)
    tok_gated = (tok_gate * tok_combined).astype(bf16)
    token_out = (activity + jnp.dot(tok_gated, w_tok_out, preferred_element_type=f32)).astype(bf16)
    return (pair_out, token_out)
```

```python
import jax
import jax.numpy as jnp
from jax import lax
from jax.sharding import PartitionSpec as P


def layer_norm(values, along_axis):
    average = jnp.mean(values, axis=along_axis, keepdims=True)
    centred = values - average
    spread = jnp.mean(centred * centred, axis=along_axis, keepdims=True)
    return centred * lax.rsqrt(spread + 1e-05)


def split_heads(values, head_count):
    return values.reshape(values.shape[:-1] + (head_count, values.shape[-1] // head_count))


def row_attention(query_rows, key_rows, value_rows, bias_block, key_shift, score_scale):
    scores = (
        jnp.einsum("jhd,khd->hjk", query_rows, key_rows, preferred_element_type=jnp.float32)
        * score_scale
    )
    scores = scores + bias_block.astype(jnp.float32) + key_shift
    weights = jax.nn.softmax(scores, axis=-1).astype(jnp.bfloat16)
    combined = jnp.einsum("hjk,khd->jhd", weights, value_rows, preferred_element_type=jnp.float32)
    return combined.reshape(combined.shape[0], -1)


def per_device(
    pair_map,
    single,
    noise_term,
    token_mask,
    w_mul_in,
    w_mul_gate,
    w_mul_out,
    w_att_in,
    w_att_bias,
    w_att_out,
    w_tok_in,
    w_pair_bias,
    w_tok_out,
):
    f32 = jnp.float32
    bf16 = jnp.bfloat16
    row_count = pair_map.shape[0]
    first_row = lax.axis_index("row") * row_count
    mask_float = token_mask.astype(f32)
    mask_rows = lax.dynamic_slice_in_dim(mask_float, first_row, row_count)
    key_shift = jnp.where(token_mask > 0, 0.0, -1000000000.0).astype(f32)
    pair_float = pair_map.astype(f32)
    normed = layer_norm(pair_float, -1).astype(bf16)
    hidden_count = w_mul_in.shape[1] // 4
    mixed = jnp.einsum("ijc,cd->dij", normed, w_mul_in, preferred_element_type=f32)
    pair_mask = mask_rows[:, None] * mask_float[None, :]
    left_side = (
        jax.nn.sigmoid(mixed[:hidden_count]) * mixed[hidden_count : 2 * hidden_count] * pair_mask
    ).astype(bf16)
    right_side = (
        jax.nn.sigmoid(mixed[2 * hidden_count : 3 * hidden_count])
        * mixed[3 * hidden_count :]
        * pair_mask
    ).astype(bf16)
    devices = lax.axis_size("row")
    tokens = pair_map.shape[1]
    part = hidden_count // devices
    activity = single.astype(f32) + noise_term.astype(f32)
    token_norm = layer_norm(activity, -1).astype(bf16)
    width_tok = single.shape[1]
    head_tok = w_pair_bias.shape[1]
    tok_projected = jnp.dot(token_norm, w_tok_in, preferred_element_type=f32)
    tok_queries = split_heads(tok_projected[:, :width_tok].astype(bf16), head_tok)
    tok_gate = jax.nn.sigmoid(tok_projected[:, 3 * width_tok :])
    kv_local = tok_projected[:, width_tok : 3 * width_tok].astype(bf16)
    sides = jnp.stack(
        [
            left_side.reshape(devices, part * row_count, tokens),
            right_side.reshape(devices, part * row_count, tokens),
        ],
        axis=1,
    ).reshape(devices, 2 * part * row_count, tokens)
    kv_block = jnp.broadcast_to(
        kv_local.reshape(1, -1, tokens), (devices, kv_local.size // tokens, tokens)
    )
    sent = jnp.concatenate([sides, kv_block], axis=1)
    got = lax.all_to_all(sent, "row", split_axis=0, concat_axis=0, tiled=True)
    sides_all = (
        got[:, : 2 * part * row_count]
        .reshape(devices, 2, part, row_count, tokens)
        .transpose(1, 2, 0, 3, 4)
        .reshape(2, part, tokens, tokens)
    )
    left_cols, right_cols = sides_all[0], sides_all[1]
    kv_all = got[:, 2 * part * row_count :].reshape(tokens, 2 * width_tok)
    crossed = jnp.einsum("cik,cjk->cij", left_cols, right_cols, preferred_element_type=f32).astype(
        bf16
    )
    crossed_rows = lax.all_to_all(crossed, "row", split_axis=1, concat_axis=0, tiled=True)
    crossed_norm = layer_norm(crossed_rows.astype(f32), 0).astype(bf16)
    update = jnp.einsum("cij,cd->ijd", crossed_norm, w_mul_out, preferred_element_type=f32)
    gating = jax.nn.sigmoid(
        jnp.einsum("ijc,cd->ijd", normed, w_mul_gate, preferred_element_type=f32)
    )
    pair_one = (pair_float + gating * update).astype(bf16)
    normed_one = layer_norm(pair_one.astype(f32), -1).astype(bf16)
    projected = jnp.einsum("ijc,cd->ijd", normed_one, w_att_in, preferred_element_type=f32)
    channels = pair_map.shape[2]
    head_tri = w_att_bias.shape[1]
    queries = split_heads(projected[..., :channels].astype(bf16), head_tri)
    keys_in = split_heads(projected[..., channels : 2 * channels].astype(bf16), head_tri)
    values_in = split_heads(projected[..., 2 * channels : 3 * channels].astype(bf16), head_tri)
    gating_att = jax.nn.sigmoid(projected[..., 3 * channels :])
    bias_local = jnp.einsum(
        "ijc,ch->hij", normed_one, w_att_bias, preferred_element_type=f32
    ).astype(bf16)
    tri_scale = (channels // head_tri) ** (-0.5)
    bias_sent = jnp.broadcast_to(bias_local[None], (devices,) + bias_local.shape)
    bias_got = lax.all_to_all(bias_sent, "row", split_axis=0, concat_axis=0, tiled=True)
    bias_all = bias_got.transpose(1, 0, 2, 3).reshape(head_tri, tokens, tokens)

    def attend_row(row_parts):
        return row_attention(
            row_parts[0], row_parts[1], row_parts[2], bias_all, key_shift, tri_scale
        )

    attended = lax.map(attend_row, (queries, keys_in, values_in))
    attended_gated = (gating_att * attended).astype(bf16)
    pair_out = (
        pair_one.astype(f32)
        + jnp.einsum("ijc,cd->ijd", attended_gated, w_att_out, preferred_element_type=f32)
    ).astype(bf16)
    tok_keys = split_heads(kv_all[:, :width_tok], head_tok)
    tok_values = split_heads(kv_all[:, width_tok:], head_tok)
    pair_norm = layer_norm(pair_out.astype(f32), -1).astype(bf16)
    pair_bias = jnp.einsum(
        "ijc,ch->hij", pair_norm, w_pair_bias, preferred_element_type=f32
    ).astype(bf16)
    tok_scale = (width_tok // head_tok) ** (-0.5)
    tok_combined = row_attention(tok_queries, tok_keys, tok_values, pair_bias, key_shift, tok_scale)
    tok_gated = (tok_gate * tok_combined).astype(bf16)
    token_out = (activity + jnp.dot(tok_gated, w_tok_out, preferred_element_type=f32)).astype(bf16)
    return (pair_out, token_out)


def solution(mesh):
    placed = (
        P(("grp", "row"), None, None),
        P(("grp", "row"), None),
        P(("grp", "row"), None),
        P("grp"),
        P(),
        P(),
        P(),
        P(),
        P(),
        P(),
        P(),
        P(),
        P(),
    )
    return jax.shard_map(
        per_device,
        mesh=mesh,
        in_specs=placed,
        out_specs=(P(("grp", "row"), None, None), P(("grp", "row"), None)),
        check_vma=False,
    )
```

```python
import functools

import jax
import jax.numpy as jnp
from jax import lax
from jax.experimental import pallas as pl
from jax.experimental.pallas import tpu as pltpu
from jax.sharding import PartitionSpec as P


def layer_norm(values, along_axis):
    average = jnp.mean(values, axis=along_axis, keepdims=True)
    centred = values - average
    spread = jnp.mean(centred * centred, axis=along_axis, keepdims=True)
    return centred * lax.rsqrt(spread + 1e-05)


def split_heads(values, head_count):
    return values.reshape(values.shape[:-1] + (head_count, values.shape[-1] // head_count))


def row_attention(query_rows, key_rows, value_rows, bias_block, key_shift, score_scale):
    scores = (
        jnp.einsum("jhd,khd->hjk", query_rows, key_rows, preferred_element_type=jnp.float32)
        * score_scale
    )
    scores = scores + bias_block.astype(jnp.float32) + key_shift
    weights = jax.nn.softmax(scores, axis=-1).astype(jnp.bfloat16)
    combined = jnp.einsum("hjk,khd->jhd", weights, value_rows, preferred_element_type=jnp.float32)
    return combined.reshape(combined.shape[0], -1)


def per_device(
    pair_map,
    single,
    noise_term,
    token_mask,
    w_mul_in,
    w_mul_gate,
    w_mul_out,
    w_att_in,
    w_att_bias,
    w_att_out,
    w_tok_in,
    w_pair_bias,
    w_tok_out,
):
    f32 = jnp.float32
    bf16 = jnp.bfloat16
    row_count = pair_map.shape[0]
    first_row = lax.axis_index("row") * row_count
    mask_float = token_mask.astype(f32)
    mask_rows = lax.dynamic_slice_in_dim(mask_float, first_row, row_count)
    key_shift = jnp.where(token_mask > 0, 0.0, -1000000000.0).astype(f32)
    pair_float = pair_map.astype(f32)
    normed = layer_norm(pair_float, -1).astype(bf16)
    hidden_count = w_mul_in.shape[1] // 4
    mixed = jnp.einsum("ijc,cd->dij", normed, w_mul_in, preferred_element_type=f32)
    pair_mask = mask_rows[:, None] * mask_float[None, :]
    left_side = (
        jax.nn.sigmoid(mixed[:hidden_count]) * mixed[hidden_count : 2 * hidden_count] * pair_mask
    ).astype(bf16)
    right_side = (
        jax.nn.sigmoid(mixed[2 * hidden_count : 3 * hidden_count])
        * mixed[3 * hidden_count :]
        * pair_mask
    ).astype(bf16)
    devices = lax.axis_size("row")
    tokens = pair_map.shape[1]
    part = hidden_count // devices
    activity = single.astype(f32) + noise_term.astype(f32)
    token_norm = layer_norm(activity, -1).astype(bf16)
    width_tok = single.shape[1]
    head_tok = w_pair_bias.shape[1]
    tok_projected = jnp.dot(token_norm, w_tok_in, preferred_element_type=f32)
    tok_queries = split_heads(tok_projected[:, :width_tok].astype(bf16), head_tok)
    tok_gate = jax.nn.sigmoid(tok_projected[:, 3 * width_tok :])
    kv_local = tok_projected[:, width_tok : 3 * width_tok].astype(bf16)
    sides = jnp.stack(
        [
            left_side.reshape(devices, part * row_count, tokens),
            right_side.reshape(devices, part * row_count, tokens),
        ],
        axis=1,
    ).reshape(devices, 2 * part * row_count, tokens)
    kv_block = jnp.broadcast_to(
        kv_local.reshape(1, -1, tokens), (devices, kv_local.size // tokens, tokens)
    )
    sent = jnp.concatenate([sides, kv_block], axis=1)
    got = lax.all_to_all(sent, "row", split_axis=0, concat_axis=0, tiled=True)
    sides_all = (
        got[:, : 2 * part * row_count]
        .reshape(devices, 2, part, row_count, tokens)
        .transpose(1, 2, 0, 3, 4)
        .reshape(2, part, tokens, tokens)
    )
    left_cols, right_cols = sides_all[0], sides_all[1]
    kv_all = got[:, 2 * part * row_count :].reshape(tokens, 2 * width_tok)
    crossed = jnp.einsum("cik,cjk->cij", left_cols, right_cols, preferred_element_type=f32).astype(
        bf16
    )
    crossed_rows = lax.all_to_all(crossed, "row", split_axis=1, concat_axis=0, tiled=True)
    crossed_norm = layer_norm(crossed_rows.astype(f32), 0).astype(bf16)
    update = jnp.einsum("cij,cd->ijd", crossed_norm, w_mul_out, preferred_element_type=f32)
    gating = jax.nn.sigmoid(
        jnp.einsum("ijc,cd->ijd", normed, w_mul_gate, preferred_element_type=f32)
    )
    pair_one = (pair_float + gating * update).astype(bf16)
    normed_one = layer_norm(pair_one.astype(f32), -1).astype(bf16)
    projected = jnp.einsum("ijc,cd->ijd", normed_one, w_att_in, preferred_element_type=f32)
    channels = pair_map.shape[2]
    head_tri = w_att_bias.shape[1]
    queries = split_heads(projected[..., :channels].astype(bf16), head_tri)
    keys_in = split_heads(projected[..., channels : 2 * channels].astype(bf16), head_tri)
    values_in = split_heads(projected[..., 2 * channels : 3 * channels].astype(bf16), head_tri)
    gating_att = jax.nn.sigmoid(projected[..., 3 * channels :])
    bias_local = jnp.einsum(
        "ijc,ch->hij", normed_one, w_att_bias, preferred_element_type=f32
    ).astype(bf16)
    tri_scale = (channels // head_tri) ** (-0.5)
    bias_sent = jnp.broadcast_to(bias_local[None], (devices,) + bias_local.shape)
    bias_got = lax.all_to_all(bias_sent, "row", split_axis=0, concat_axis=0, tiled=True)
    bias_all = bias_got.transpose(1, 0, 2, 3).reshape(head_tri, tokens, tokens)

    def attend_row(row_parts):
        return row_attention(
            row_parts[0], row_parts[1], row_parts[2], bias_all, key_shift, tri_scale
        )

    attended = lax.map(attend_row, (queries, keys_in, values_in))
    attended_gated = (gating_att * attended).astype(bf16)
    pair_out = (
        pair_one.astype(f32)
        + jnp.einsum("ijc,cd->ijd", attended_gated, w_att_out, preferred_element_type=f32)
    ).astype(bf16)
    tok_keys = split_heads(kv_all[:, :width_tok], head_tok)
    tok_values = split_heads(kv_all[:, width_tok:], head_tok)
    pair_norm = layer_norm(pair_out.astype(f32), -1).astype(bf16)
    pair_bias = jnp.einsum(
        "ijc,ch->hij", pair_norm, w_pair_bias, preferred_element_type=f32
    ).astype(bf16)
    tok_scale = (width_tok // head_tok) ** (-0.5)
    tok_combined = row_attention(tok_queries, tok_keys, tok_values, pair_bias, key_shift, tok_scale)
    tok_gated = (tok_gate * tok_combined).astype(bf16)
    token_out = (activity + jnp.dot(tok_gated, w_tok_out, preferred_element_type=f32)).astype(bf16)
    return (pair_out, token_out)


def dot_nn(a, b):
    return lax.dot_general(a, b, (((1,), (0,)), ((), ())), preferred_element_type=jnp.float32)


def dot_nt(a, b):
    return lax.dot_general(a, b, (((1,), (1,)), ((), ())), preferred_element_type=jnp.float32)


def lane_norm(values):
    return layer_norm(values, -1).astype(jnp.bfloat16)


def softmax_rows(scores):
    shifted = jnp.exp(scores - jnp.max(scores, axis=-1, keepdims=True))
    return (shifted * (1.0 / jnp.sum(shifted, axis=-1, keepdims=True))).astype(jnp.bfloat16)


def fused_kernel(
    devices,
    mask_scalar,
    mask_lane,
    pair_ref,
    single_ref,
    noise_ref,
    w_sides,
    w_mul_gate,
    w_mul_out,
    w_att_in,
    w_small,
    w_att_out,
    w_tok_in,
    w_tok_out,
    pair_out,
    token_out,
    send_sides,
    recv_sides,
    send_prod,
    recv_prod,
    send_bias,
    recv_bias,
    send_kv,
    recv_kv,
    wide_sides,
    wide_prod,
    wide_back,
    wide_bias,
    wide_all,
    wide_kv,
    wide_keys,
    send_sem,
    recv_sem,
):
    f32 = jnp.float32
    bf16 = jnp.bfloat16
    me = lax.axis_index("row")

    barrier = pltpu.get_barrier_semaphore()

    def greet(step, carry):
        other = lax.rem(me + step, devices)
        pl.semaphore_signal(
            barrier, inc=1, device_id={"row": other}, device_id_type=pl.DeviceIdType.MESH
        )
        return carry

    lax.fori_loop(1, devices, greet, 0)

    def send_all(slot, source, landing):
        def one(step, carry):
            other = lax.rem(me + step, devices)
            pltpu.make_async_remote_copy(
                src_ref=source(other),
                dst_ref=landing.at[me],
                send_sem=send_sem.at[slot],
                recv_sem=recv_sem.at[slot],
                device_id={"row": other},
                device_id_type=pl.DeviceIdType.MESH,
            ).start()
            return carry

        lax.fori_loop(1, devices, one, 0)

    def wait_all(sem, landing):
        whole = landing.at[pl.ds(0, devices - 1)]
        pltpu.make_async_copy(whole, whole, sem).wait()

    pair = pair_ref[...].astype(f32)
    normed = lane_norm(pair)
    mixed = dot_nt(w_sides[...], normed)
    mask = mask_lane[...].astype(f32)
    half = w_sides.shape[0] // 2
    blocks = []
    for i in range(4):
        mask_row = mask_scalar[me * 4 + i].astype(f32)
        cols = slice(i * 128, (i + 1) * 128)
        side = jax.nn.sigmoid(mixed[:half, cols]) * mixed[half:, cols] * (mask * mask_row)
        blocks.append(side.reshape(devices, 8, 128))
    send_sides[...] = jnp.concatenate(blocks, axis=1).astype(bf16)
    recv_sides[me] = send_sides[me]
    pl.semaphore_wait(barrier, devices - 1)
    send_all(0, lambda other: send_sides.at[other], recv_sides)

    activity = single_ref[...].astype(f32) + noise_ref[...].astype(f32)
    activity = jnp.concatenate([activity, jnp.zeros_like(activity)], axis=0)
    tok = dot_nn(lane_norm(activity), w_tok_in[...])
    width = single_ref.shape[1]
    wide_kv[...] = jnp.zeros_like(wide_kv)
    for m in range(6):
        wide_kv[pl.ds(m, 4, stride=8), :] = tok[:4, width + m * 128 : width + (m + 1) * 128]
    send_kv[...] = wide_kv[...].astype(bf16)
    recv_kv[me] = send_kv[...]
    gating = jax.nn.sigmoid(dot_nn(normed, w_mul_gate[...]))

    wait_all(recv_sem.at[0], recv_sides)
    wide_sides[...] = recv_sides[...].astype(f32).reshape(wide_sides.shape)
    for c in range(4):
        left = wide_sides[pl.ds(c, 128, stride=8), :].astype(bf16)
        right = wide_sides[pl.ds(4 + c, 128, stride=8), :].astype(bf16)
        wide_prod[pl.ds(c, 128, stride=4), :] = dot_nt(left, right)
    send_prod[...] = wide_prod[...].astype(bf16).reshape(send_prod.shape)
    recv_prod[me] = send_prod[me]
    send_all(1, lambda other: send_prod.at[other], recv_prod)
    send_all(3, lambda other: send_kv, recv_kv)
    wait_all(recv_sem.at[1], recv_prod)
    wide_back[...] = recv_prod[...].astype(f32).reshape(wide_back.shape)
    crossed_norm = []
    for i in range(4):
        crossed = jnp.concatenate(
            [wide_back[pl.ds(i * 4 + c, devices, stride=16), :] for c in range(4)], axis=0
        )
        crossed_norm.append(layer_norm(crossed, 0).T.astype(bf16))
    update = dot_nn(jnp.concatenate(crossed_norm, axis=0), w_mul_out[...])
    pair_one = (pair + gating * update).astype(bf16).astype(f32)

    normed_one = lane_norm(pair_one)
    bias = dot_nt(w_small[16:32], normed_one)
    for i in range(4):
        wide_bias[i * 4 : (i + 1) * 4, :] = bias[:4, i * 128 : (i + 1) * 128]
    send_bias[...] = wide_bias[...].astype(bf16)
    recv_bias[me] = send_bias[...]
    send_all(2, lambda other: send_bias, recv_bias)
    projected = dot_nn(normed_one, w_att_in[...])
    shift = jnp.where(mask > 0, 0.0, -1000000000.0).astype(f32)
    head_of = lax.broadcasted_iota(jnp.int32, (128, 128), 1) // 32
    raw = []
    for i in range(4):
        rows = slice(i * 128, (i + 1) * 128)
        query = projected[rows, :128]
        query = jnp.concatenate([jnp.where(head_of == h, query, 0.0) for h in range(4)], axis=0)
        raw.append(dot_nt(query.astype(bf16), projected[rows, 128:256].astype(bf16)))

    wait_all(recv_sem.at[2], recv_bias)
    wide_all[...] = recv_bias[...].astype(f32).reshape(wide_all.shape)
    bias_all = jnp.concatenate(
        [wide_all[pl.ds(h, 128, stride=4), :] for h in range(4)], axis=0
    )
    scale = 32.0**-0.5
    gated = []
    for i in range(4):
        rows = slice(i * 128, (i + 1) * 128)
        weights = softmax_rows(raw[i] * scale + bias_all + shift)
        spread = dot_nn(weights, projected[rows, 256:384].astype(bf16))
        attended = jnp.zeros((128, 128), f32)
        for h in range(4):
            attended = jnp.where(head_of == h, spread[h * 128 : (h + 1) * 128], attended)
        gated.append((jax.nn.sigmoid(projected[rows, 384:]) * attended).astype(bf16))
    final = (pair_one + dot_nn(jnp.concatenate(gated, axis=0), w_att_out[...])).astype(bf16)
    pair_out[...] = final

    pair_bias = dot_nt(w_small[0:16], lane_norm(final.astype(f32))).astype(bf16).astype(f32)
    pair_bias = jnp.concatenate([pair_bias[:, i * 128 : (i + 1) * 128] for i in range(4)], axis=0)
    lane = lax.broadcasted_iota(jnp.int32, (16, width), 1)
    head = lax.broadcasted_iota(jnp.int32, (16, width), 0)
    own = (lane >= head * 24) & (lane < head * 24 + 24)
    query = jnp.concatenate([jnp.where(own, tok[i : i + 1, :width], 0.0) for i in range(4)], axis=0)
    wait_all(recv_sem.at[3], recv_kv)
    wide_keys[...] = recv_kv[...].astype(f32).reshape(wide_keys.shape)
    chunks = [wide_keys[pl.ds(m, 128, stride=8), :].astype(bf16) for m in range(6)]
    keys = jnp.concatenate(chunks[:3], axis=1)
    values = jnp.concatenate(chunks[3:], axis=1)
    weights = softmax_rows(dot_nt(query.astype(bf16), keys) * 24.0**-0.5 + pair_bias + shift)
    spread = dot_nn(weights, values)
    combined = jnp.concatenate(
        [
            jnp.sum(jnp.where(own, spread[i * 16 : (i + 1) * 16], 0.0), axis=0, keepdims=True)
            for i in range(4)
        ]
        + [jnp.zeros((4, width), f32)],
        axis=0,
    )
    tok_gated = (jax.nn.sigmoid(tok[:, 3 * width :]) * combined).astype(bf16)
    token_out[...] = (activity + dot_nn(tok_gated, w_tok_out[...]))[:4].astype(bf16)

    wait_all(send_sem.at[0], recv_sides)
    wait_all(send_sem.at[1], recv_prod)
    wait_all(send_sem.at[2], recv_bias)
    wait_all(send_sem.at[3], recv_kv)


def fused(
    pair_map,
    single,
    noise_term,
    token_mask,
    w_mul_in,
    w_mul_gate,
    w_mul_out,
    w_att_in,
    w_att_bias,
    w_att_out,
    w_tok_in,
    w_pair_bias,
    w_tok_out,
):
    bf16 = jnp.bfloat16
    f32 = jnp.float32
    devices = lax.axis_size("row")
    w_sides = (
        w_mul_in.T.reshape(2, 2, devices, 4, 128).transpose(1, 2, 0, 3, 4).reshape(512, 128)
    )
    w_back = w_mul_out.reshape(devices, 4, 128).transpose(1, 0, 2).reshape(128, 128)
    w_small = jnp.concatenate([w_pair_bias.T, w_att_bias.T, jnp.zeros((12, 128), bf16)], axis=0)
    vmem = pl.BlockSpec(memory_space=pltpu.VMEM)
    pair_out, token_out = pl.pallas_call(
        functools.partial(fused_kernel, devices),
        out_shape=(
            jax.ShapeDtypeStruct((512, 128), bf16),
            jax.ShapeDtypeStruct(single.shape, bf16),
        ),
        in_specs=[pl.BlockSpec(memory_space=pltpu.SMEM)] + [vmem] * 12,
        out_specs=(vmem, vmem),
        scratch_shapes=[
            pltpu.VMEM((devices, 32, 128), bf16),
            pltpu.VMEM((devices, 32, 128), bf16),
            pltpu.VMEM((devices, 16, 128), bf16),
            pltpu.VMEM((devices, 16, 128), bf16),
            pltpu.VMEM((16, 128), bf16),
            pltpu.VMEM((devices, 16, 128), bf16),
            pltpu.VMEM((32, 128), bf16),
            pltpu.VMEM((devices, 32, 128), bf16),
            pltpu.VMEM((devices * 32, 128), f32),
            pltpu.VMEM((devices * 16, 128), f32),
            pltpu.VMEM((devices * 16, 128), f32),
            pltpu.VMEM((16, 128), f32),
            pltpu.VMEM((devices * 16, 128), f32),
            pltpu.VMEM((32, 128), f32),
            pltpu.VMEM((devices * 32, 128), f32),
            pltpu.SemaphoreType.DMA((4,)),
            pltpu.SemaphoreType.DMA((4,)),
        ],
        compiler_params=pltpu.CompilerParams(
            collective_id=0, has_side_effects=True, vmem_limit_bytes=40 * 1024 * 1024
        ),
    )(
        token_mask,
        token_mask.reshape(1, -1),
        pair_map.reshape(512, 128),
        single,
        noise_term,
        w_sides,
        w_mul_gate,
        w_back,
        w_att_in,
        w_small,
        w_att_out,
        w_tok_in,
        w_tok_out,
    )
    return pair_out.reshape(pair_map.shape), token_out


def solution(mesh):
    placed = (
        P(("grp", "row"), None, None),
        P(("grp", "row"), None),
        P(("grp", "row"), None),
        P("grp"),
        P(),
        P(),
        P(),
        P(),
        P(),
        P(),
        P(),
        P(),
        P(),
    )

    def body(*arrays):
        devices = mesh.shape["row"]
        fits = arrays[0].shape == (4, 128, 128) and devices == 32
        fits = fits and arrays[1].shape[1] == 384 and arrays[4].shape[1] == 512
        return fused(*arrays) if fits else per_device(*arrays)

    return jax.shard_map(
        body,
        mesh=mesh,
        in_specs=placed,
        out_specs=(P(("grp", "row"), None, None), P(("grp", "row"), None)),
        check_vma=False,
    )
```

```python
import functools

import jax
import jax.numpy as jnp
from jax import lax
from jax.experimental import pallas as pl
from jax.experimental.pallas import tpu as pltpu
from jax.sharding import PartitionSpec as P


def layer_norm(values, along_axis):
    average = jnp.mean(values, axis=along_axis, keepdims=True)
    centred = values - average
    spread = jnp.mean(centred * centred, axis=along_axis, keepdims=True)
    return centred * lax.rsqrt(spread + 1e-05)


def split_heads(values, head_count):
    return values.reshape(values.shape[:-1] + (head_count, values.shape[-1] // head_count))


def row_attention(query_rows, key_rows, value_rows, bias_block, key_shift, score_scale):
    scores = (
        jnp.einsum("jhd,khd->hjk", query_rows, key_rows, preferred_element_type=jnp.float32)
        * score_scale
    )
    scores = scores + bias_block.astype(jnp.float32) + key_shift
    weights = jax.nn.softmax(scores, axis=-1).astype(jnp.bfloat16)
    combined = jnp.einsum("hjk,khd->jhd", weights, value_rows, preferred_element_type=jnp.float32)
    return combined.reshape(combined.shape[0], -1)


def per_device(
    pair_map,
    single,
    noise_term,
    token_mask,
    w_mul_in,
    w_mul_gate,
    w_mul_out,
    w_att_in,
    w_att_bias,
    w_att_out,
    w_tok_in,
    w_pair_bias,
    w_tok_out,
):
    f32 = jnp.float32
    bf16 = jnp.bfloat16
    row_count = pair_map.shape[0]
    first_row = lax.axis_index("row") * row_count
    mask_float = token_mask.astype(f32)
    mask_rows = lax.dynamic_slice_in_dim(mask_float, first_row, row_count)
    key_shift = jnp.where(token_mask > 0, 0.0, -1000000000.0).astype(f32)
    pair_float = pair_map.astype(f32)
    normed = layer_norm(pair_float, -1).astype(bf16)
    hidden_count = w_mul_in.shape[1] // 4
    mixed = jnp.einsum("ijc,cd->dij", normed, w_mul_in, preferred_element_type=f32)
    pair_mask = mask_rows[:, None] * mask_float[None, :]
    left_side = (
        jax.nn.sigmoid(mixed[:hidden_count]) * mixed[hidden_count : 2 * hidden_count] * pair_mask
    ).astype(bf16)
    right_side = (
        jax.nn.sigmoid(mixed[2 * hidden_count : 3 * hidden_count])
        * mixed[3 * hidden_count :]
        * pair_mask
    ).astype(bf16)
    devices = lax.axis_size("row")
    tokens = pair_map.shape[1]
    part = hidden_count // devices
    activity = single.astype(f32) + noise_term.astype(f32)
    token_norm = layer_norm(activity, -1).astype(bf16)
    width_tok = single.shape[1]
    head_tok = w_pair_bias.shape[1]
    tok_projected = jnp.dot(token_norm, w_tok_in, preferred_element_type=f32)
    tok_queries = split_heads(tok_projected[:, :width_tok].astype(bf16), head_tok)
    tok_gate = jax.nn.sigmoid(tok_projected[:, 3 * width_tok :])
    kv_local = tok_projected[:, width_tok : 3 * width_tok].astype(bf16)
    sides = jnp.stack(
        [
            left_side.reshape(devices, part * row_count, tokens),
            right_side.reshape(devices, part * row_count, tokens),
        ],
        axis=1,
    ).reshape(devices, 2 * part * row_count, tokens)
    kv_block = jnp.broadcast_to(
        kv_local.reshape(1, -1, tokens), (devices, kv_local.size // tokens, tokens)
    )
    sent = jnp.concatenate([sides, kv_block], axis=1)
    got = lax.all_to_all(sent, "row", split_axis=0, concat_axis=0, tiled=True)
    sides_all = (
        got[:, : 2 * part * row_count]
        .reshape(devices, 2, part, row_count, tokens)
        .transpose(1, 2, 0, 3, 4)
        .reshape(2, part, tokens, tokens)
    )
    left_cols, right_cols = sides_all[0], sides_all[1]
    kv_all = got[:, 2 * part * row_count :].reshape(tokens, 2 * width_tok)
    crossed = jnp.einsum("cik,cjk->cij", left_cols, right_cols, preferred_element_type=f32).astype(
        bf16
    )
    crossed_rows = lax.all_to_all(crossed, "row", split_axis=1, concat_axis=0, tiled=True)
    crossed_norm = layer_norm(crossed_rows.astype(f32), 0).astype(bf16)
    update = jnp.einsum("cij,cd->ijd", crossed_norm, w_mul_out, preferred_element_type=f32)
    gating = jax.nn.sigmoid(
        jnp.einsum("ijc,cd->ijd", normed, w_mul_gate, preferred_element_type=f32)
    )
    pair_one = (pair_float + gating * update).astype(bf16)
    normed_one = layer_norm(pair_one.astype(f32), -1).astype(bf16)
    projected = jnp.einsum("ijc,cd->ijd", normed_one, w_att_in, preferred_element_type=f32)
    channels = pair_map.shape[2]
    head_tri = w_att_bias.shape[1]
    queries = split_heads(projected[..., :channels].astype(bf16), head_tri)
    keys_in = split_heads(projected[..., channels : 2 * channels].astype(bf16), head_tri)
    values_in = split_heads(projected[..., 2 * channels : 3 * channels].astype(bf16), head_tri)
    gating_att = jax.nn.sigmoid(projected[..., 3 * channels :])
    bias_local = jnp.einsum(
        "ijc,ch->hij", normed_one, w_att_bias, preferred_element_type=f32
    ).astype(bf16)
    tri_scale = (channels // head_tri) ** (-0.5)
    bias_sent = jnp.broadcast_to(bias_local[None], (devices,) + bias_local.shape)
    bias_got = lax.all_to_all(bias_sent, "row", split_axis=0, concat_axis=0, tiled=True)
    bias_all = bias_got.transpose(1, 0, 2, 3).reshape(head_tri, tokens, tokens)

    def attend_row(row_parts):
        return row_attention(
            row_parts[0], row_parts[1], row_parts[2], bias_all, key_shift, tri_scale
        )

    attended = lax.map(attend_row, (queries, keys_in, values_in))
    attended_gated = (gating_att * attended).astype(bf16)
    pair_out = (
        pair_one.astype(f32)
        + jnp.einsum("ijc,cd->ijd", attended_gated, w_att_out, preferred_element_type=f32)
    ).astype(bf16)
    tok_keys = split_heads(kv_all[:, :width_tok], head_tok)
    tok_values = split_heads(kv_all[:, width_tok:], head_tok)
    pair_norm = layer_norm(pair_out.astype(f32), -1).astype(bf16)
    pair_bias = jnp.einsum(
        "ijc,ch->hij", pair_norm, w_pair_bias, preferred_element_type=f32
    ).astype(bf16)
    tok_scale = (width_tok // head_tok) ** (-0.5)
    tok_combined = row_attention(tok_queries, tok_keys, tok_values, pair_bias, key_shift, tok_scale)
    tok_gated = (tok_gate * tok_combined).astype(bf16)
    token_out = (activity + jnp.dot(tok_gated, w_tok_out, preferred_element_type=f32)).astype(bf16)
    return (pair_out, token_out)


def dot_nn(a, b):
    return lax.dot_general(a, b, (((1,), (0,)), ((), ())), preferred_element_type=jnp.float32)


def dot_nt(a, b):
    return lax.dot_general(a, b, (((1,), (1,)), ((), ())), preferred_element_type=jnp.float32)


def lane_norm(values):
    return layer_norm(values, -1).astype(jnp.bfloat16)


def softmax_rows(scores):
    shifted = jnp.exp(scores - jnp.max(scores, axis=-1, keepdims=True))
    return (shifted * (1.0 / jnp.sum(shifted, axis=-1, keepdims=True))).astype(jnp.bfloat16)


def fused_kernel(
    devices,
    *refs,
):
    operands, (pair_out, token_out), refs = refs[:13], refs[13:15], refs[15:]
    held, local_sem, refs = refs[:13], refs[13], refs[14:]
    kernel_body(devices, operands, held, local_sem, pair_out, token_out, *refs)


def kernel_body(
    devices,
    operands,
    held,
    local_sem,
    pair_out,
    token_out,
    send_sides,
    recv_sides,
    send_prod,
    recv_prod,
    send_bias,
    recv_bias,
    send_kv,
    recv_kv,
    wide_sides,
    wide_prod,
    wide_back,
    wide_bias,
    wide_all,
    wide_kv,
    wide_keys,
    wide_w,
    w_sides,
    wide_out,
    send_sem,
    recv_sem,
):
    f32 = jnp.float32
    bf16 = jnp.bfloat16
    me = lax.axis_index("row")
    (
        pair_ref,
        single_ref,
        noise_ref,
        mask_lane,
        w_mul_in,
        w_mul_gate,
        w_mul_out,
        w_att_in,
        w_att_bias,
        w_att_out,
        w_tok_in,
        w_pair_bias,
        w_tok_out,
    ) = held
    loads = [
        pltpu.make_async_copy(source, target, local_sem.at[index])
        for index, (source, target) in enumerate(zip(operands, held))
    ]
    for index in (0, 4, 3, 1, 2, 10, 5, 6, 7, 8, 9, 11, 12):
        loads[index].start()

    barrier = pltpu.get_barrier_semaphore()

    def greet(step, carry):
        other = lax.rem(me + step, devices)
        pl.semaphore_signal(
            barrier, inc=1, device_id={"row": other}, device_id_type=pl.DeviceIdType.MESH
        )
        return carry

    lax.fori_loop(1, devices, greet, 0)

    def send_all(slot, source, landing):
        def one(step, carry):
            other = lax.rem(me + step, devices)
            pltpu.make_async_remote_copy(
                src_ref=source(other),
                dst_ref=landing.at[me],
                send_sem=send_sem.at[slot],
                recv_sem=recv_sem.at[slot],
                device_id={"row": other},
                device_id_type=pl.DeviceIdType.MESH,
            ).start()
            return carry

        lax.fori_loop(1, devices, one, 0)

    def wait_all(sem, landing):
        whole = landing.at[pl.ds(0, devices - 1)]
        pltpu.make_async_copy(whole, whole, sem).wait()

    loads[4].wait()
    wide_w[...] = w_mul_in[...].astype(f32).T
    for kind in range(4):
        for c in range(4):
            w_sides[pl.ds((kind % 2) * 256 + (kind // 2) * 4 + c, devices, stride=8), :] = wide_w[
                pl.ds(kind * 128 + c, devices, stride=4), :
            ]
    loads[0].wait()
    loads[3].wait()
    pair = pair_ref[...].astype(f32)
    normed = lane_norm(pair)
    mixed = dot_nt(w_sides[...].astype(bf16), normed)
    mask = mask_lane[...].astype(f32)
    place = lax.broadcasted_iota(jnp.int32, mask.shape, 1)
    half = w_sides.shape[0] // 2
    blocks = []
    for i in range(4):
        mask_row = jnp.sum(jnp.where(place == me * 4 + i, mask, 0.0), axis=1, keepdims=True)
        cols = slice(i * 128, (i + 1) * 128)
        side = jax.nn.sigmoid(mixed[:half, cols]) * mixed[half:, cols] * (mask * mask_row)
        blocks.append(side.reshape(devices, 8, 128))
    send_sides[...] = jnp.concatenate(blocks, axis=1).astype(bf16)
    recv_sides[me] = send_sides[me]
    pl.semaphore_wait(barrier, devices - 1)
    send_all(0, lambda other: send_sides.at[other], recv_sides)

    for index in (1, 2, 10):
        loads[index].wait()
    activity = single_ref[...].astype(f32) + noise_ref[...].astype(f32)
    activity = jnp.concatenate([activity, jnp.zeros_like(activity)], axis=0)
    tok = dot_nn(lane_norm(activity), w_tok_in[...])
    width = single_ref.shape[1]
    wide_kv[...] = jnp.zeros_like(wide_kv)
    for m in range(6):
        wide_kv[pl.ds(m, 4, stride=8), :] = tok[:4, width + m * 128 : width + (m + 1) * 128]
    send_kv[...] = wide_kv[...].astype(bf16)
    recv_kv[me] = send_kv[...]
    for index in (5, 6, 7, 8, 9, 11, 12):
        loads[index].wait()
    gating = jax.nn.sigmoid(dot_nn(normed, w_mul_gate[...]))
    wide_out[...] = w_mul_out[...].astype(f32)
    w_back = jnp.concatenate(
        [wide_out[pl.ds(c, devices, stride=4), :] for c in range(4)], axis=0
    ).astype(bf16)
    w_att_bias_t = jnp.concatenate(
        [w_att_bias[...].astype(f32), jnp.zeros((12, 128), f32)], axis=0
    ).astype(bf16)

    wait_all(recv_sem.at[0], recv_sides)
    wide_sides[...] = recv_sides[...].astype(f32).reshape(wide_sides.shape)
    for c in range(4):
        left = wide_sides[pl.ds(c, 128, stride=8), :].astype(bf16)
        right = wide_sides[pl.ds(4 + c, 128, stride=8), :].astype(bf16)
        wide_prod[pl.ds(c, 128, stride=4), :] = dot_nt(left, right)
    send_prod[...] = wide_prod[...].astype(bf16).reshape(send_prod.shape)
    recv_prod[me] = send_prod[me]
    send_all(1, lambda other: send_prod.at[other], recv_prod)
    send_all(3, lambda other: send_kv, recv_kv)
    wait_all(recv_sem.at[1], recv_prod)
    wide_back[...] = recv_prod[...].astype(f32).reshape(wide_back.shape)
    crossed_norm = []
    for i in range(4):
        crossed = jnp.concatenate(
            [wide_back[pl.ds(i * 4 + c, devices, stride=16), :] for c in range(4)], axis=0
        )
        crossed_norm.append(layer_norm(crossed, 0).T.astype(bf16))
    update = dot_nn(jnp.concatenate(crossed_norm, axis=0), w_back)
    pair_one = (pair + gating * update).astype(bf16).astype(f32)

    normed_one = lane_norm(pair_one)
    bias = dot_nt(w_att_bias_t, normed_one)
    for i in range(4):
        wide_bias[i * 4 : (i + 1) * 4, :] = bias[:4, i * 128 : (i + 1) * 128]
    send_bias[...] = wide_bias[...].astype(bf16)
    recv_bias[me] = send_bias[...]
    send_all(2, lambda other: send_bias, recv_bias)
    projected = dot_nn(normed_one, w_att_in[...])
    shift = jnp.where(mask > 0, 0.0, -1000000000.0).astype(f32)
    head_of = lax.broadcasted_iota(jnp.int32, (128, 128), 1) // 32
    raw = []
    for i in range(4):
        rows = slice(i * 128, (i + 1) * 128)
        query = projected[rows, :128]
        query = jnp.concatenate([jnp.where(head_of == h, query, 0.0) for h in range(4)], axis=0)
        raw.append(dot_nt(query.astype(bf16), projected[rows, 128:256].astype(bf16)))

    wait_all(recv_sem.at[2], recv_bias)
    wide_all[...] = recv_bias[...].astype(f32).reshape(wide_all.shape)
    bias_all = jnp.concatenate(
        [wide_all[pl.ds(h, 128, stride=4), :] for h in range(4)], axis=0
    )
    scale = 32.0**-0.5
    gated = []
    for i in range(4):
        rows = slice(i * 128, (i + 1) * 128)
        weights = softmax_rows(raw[i] * scale + bias_all + shift)
        spread = dot_nn(weights, projected[rows, 256:384].astype(bf16))
        attended = jnp.zeros((128, 128), f32)
        for h in range(4):
            attended = jnp.where(head_of == h, spread[h * 128 : (h + 1) * 128], attended)
        gated.append((jax.nn.sigmoid(projected[rows, 384:]) * attended).astype(bf16))
    final = (pair_one + dot_nn(jnp.concatenate(gated, axis=0), w_att_out[...])).astype(bf16)
    pair_out[...] = final

    pair_bias = dot_nt(w_pair_bias[...], lane_norm(final.astype(f32))).astype(bf16).astype(f32)
    pair_bias = jnp.concatenate([pair_bias[:, i * 128 : (i + 1) * 128] for i in range(4)], axis=0)
    lane = lax.broadcasted_iota(jnp.int32, (16, width), 1)
    head = lax.broadcasted_iota(jnp.int32, (16, width), 0)
    own = (lane >= head * 24) & (lane < head * 24 + 24)
    query = jnp.concatenate([jnp.where(own, tok[i : i + 1, :width], 0.0) for i in range(4)], axis=0)
    wait_all(recv_sem.at[3], recv_kv)
    wide_keys[...] = recv_kv[...].astype(f32).reshape(wide_keys.shape)
    chunks = [wide_keys[pl.ds(m, 128, stride=8), :].astype(bf16) for m in range(6)]
    keys = jnp.concatenate(chunks[:3], axis=1)
    values = jnp.concatenate(chunks[3:], axis=1)
    weights = softmax_rows(dot_nt(query.astype(bf16), keys) * 24.0**-0.5 + pair_bias + shift)
    spread = dot_nn(weights, values)
    combined = jnp.concatenate(
        [
            jnp.sum(jnp.where(own, spread[i * 16 : (i + 1) * 16], 0.0), axis=0, keepdims=True)
            for i in range(4)
        ]
        + [jnp.zeros((4, width), f32)],
        axis=0,
    )
    tok_gated = (jax.nn.sigmoid(tok[:, 3 * width :]) * combined).astype(bf16)
    token_out[...] = (activity + dot_nn(tok_gated, w_tok_out[...]))[:4].astype(bf16)

    wait_all(send_sem.at[0], recv_sides)
    wait_all(send_sem.at[1], recv_prod)
    wait_all(send_sem.at[2], recv_bias)
    wait_all(send_sem.at[3], recv_kv)


def fused(
    pair_map,
    single,
    noise_term,
    token_mask,
    w_mul_in,
    w_mul_gate,
    w_mul_out,
    w_att_in,
    w_att_bias,
    w_att_out,
    w_tok_in,
    w_pair_bias,
    w_tok_out,
):
    bf16 = jnp.bfloat16
    f32 = jnp.float32
    devices = lax.axis_size("row")
    operands = (
        pair_map.reshape(512, 128),
        single,
        noise_term,
        token_mask.reshape(1, -1),
        w_mul_in,
        w_mul_gate,
        w_mul_out,
        w_att_in,
        w_att_bias.T,
        w_att_out,
        w_tok_in,
        w_pair_bias.T,
        w_tok_out,
    )
    vmem = pl.BlockSpec(memory_space=pltpu.VMEM)
    pair_out, token_out = pl.pallas_call(
        functools.partial(fused_kernel, devices),
        out_shape=(
            jax.ShapeDtypeStruct((512, 128), bf16),
            jax.ShapeDtypeStruct(single.shape, bf16),
        ),
        in_specs=[pl.BlockSpec(memory_space=pl.ANY)] * 13,
        out_specs=(vmem, vmem),
        scratch_shapes=[pltpu.VMEM(held.shape, held.dtype) for held in operands]
        + [
            pltpu.SemaphoreType.DMA((13,)),
            pltpu.VMEM((devices, 32, 128), bf16),
            pltpu.VMEM((devices, 32, 128), bf16),
            pltpu.VMEM((devices, 16, 128), bf16),
            pltpu.VMEM((devices, 16, 128), bf16),
            pltpu.VMEM((16, 128), bf16),
            pltpu.VMEM((devices, 16, 128), bf16),
            pltpu.VMEM((32, 128), bf16),
            pltpu.VMEM((devices, 32, 128), bf16),
            pltpu.VMEM((devices * 32, 128), f32),
            pltpu.VMEM((devices * 16, 128), f32),
            pltpu.VMEM((devices * 16, 128), f32),
            pltpu.VMEM((16, 128), f32),
            pltpu.VMEM((devices * 16, 128), f32),
            pltpu.VMEM((32, 128), f32),
            pltpu.VMEM((devices * 32, 128), f32),
            pltpu.VMEM((512, 128), f32),
            pltpu.VMEM((512, 128), f32),
            pltpu.VMEM((128, 128), f32),
            pltpu.SemaphoreType.DMA((4,)),
            pltpu.SemaphoreType.DMA((4,)),
        ],
        compiler_params=pltpu.CompilerParams(
            collective_id=0, has_side_effects=True, vmem_limit_bytes=56 * 1024 * 1024
        ),
    )(*operands)
    return pair_out.reshape(pair_map.shape), token_out


def solution(mesh):
    placed = (
        P(("grp", "row"), None, None),
        P(("grp", "row"), None),
        P(("grp", "row"), None),
        P("grp"),
        P(),
        P(),
        P(),
        P(),
        P(),
        P(),
        P(),
        P(),
        P(),
    )

    def body(*arrays):
        devices = mesh.shape["row"]
        fits = arrays[0].shape == (4, 128, 128) and devices == 32
        fits = fits and arrays[1].shape[1] == 384 and arrays[4].shape[1] == 512
        return fused(*arrays) if fits else per_device(*arrays)

    return jax.shard_map(
        body,
        mesh=mesh,
        in_specs=placed,
        out_specs=(P(("grp", "row"), None, None), P(("grp", "row"), None)),
        check_vma=False,
    )
```

```python
import functools

import jax
import jax.numpy as jnp
from jax import lax
from jax.experimental import pallas as pl
from jax.experimental.pallas import tpu as pltpu
from jax.sharding import PartitionSpec as P


def layer_norm(values, along_axis):
    average = jnp.mean(values, axis=along_axis, keepdims=True)
    centred = values - average
    spread = jnp.mean(centred * centred, axis=along_axis, keepdims=True)
    return centred * lax.rsqrt(spread + 1e-05)


def split_heads(values, head_count):
    return values.reshape(values.shape[:-1] + (head_count, values.shape[-1] // head_count))


def row_attention(query_rows, key_rows, value_rows, bias_block, key_shift, score_scale):
    scores = (
        jnp.einsum("jhd,khd->hjk", query_rows, key_rows, preferred_element_type=jnp.float32)
        * score_scale
    )
    scores = scores + bias_block.astype(jnp.float32) + key_shift
    weights = jax.nn.softmax(scores, axis=-1).astype(jnp.bfloat16)
    combined = jnp.einsum("hjk,khd->jhd", weights, value_rows, preferred_element_type=jnp.float32)
    return combined.reshape(combined.shape[0], -1)


def per_device(
    pair_map,
    single,
    noise_term,
    token_mask,
    w_mul_in,
    w_mul_gate,
    w_mul_out,
    w_att_in,
    w_att_bias,
    w_att_out,
    w_tok_in,
    w_pair_bias,
    w_tok_out,
):
    f32 = jnp.float32
    bf16 = jnp.bfloat16
    row_count = pair_map.shape[0]
    first_row = lax.axis_index("row") * row_count
    mask_float = token_mask.astype(f32)
    mask_rows = lax.dynamic_slice_in_dim(mask_float, first_row, row_count)
    key_shift = jnp.where(token_mask > 0, 0.0, -1000000000.0).astype(f32)
    pair_float = pair_map.astype(f32)
    normed = layer_norm(pair_float, -1).astype(bf16)
    hidden_count = w_mul_in.shape[1] // 4
    mixed = jnp.einsum("ijc,cd->dij", normed, w_mul_in, preferred_element_type=f32)
    pair_mask = mask_rows[:, None] * mask_float[None, :]
    left_side = (
        jax.nn.sigmoid(mixed[:hidden_count]) * mixed[hidden_count : 2 * hidden_count] * pair_mask
    ).astype(bf16)
    right_side = (
        jax.nn.sigmoid(mixed[2 * hidden_count : 3 * hidden_count])
        * mixed[3 * hidden_count :]
        * pair_mask
    ).astype(bf16)
    devices = lax.axis_size("row")
    tokens = pair_map.shape[1]
    part = hidden_count // devices
    activity = single.astype(f32) + noise_term.astype(f32)
    token_norm = layer_norm(activity, -1).astype(bf16)
    width_tok = single.shape[1]
    head_tok = w_pair_bias.shape[1]
    tok_projected = jnp.dot(token_norm, w_tok_in, preferred_element_type=f32)
    tok_queries = split_heads(tok_projected[:, :width_tok].astype(bf16), head_tok)
    tok_gate = jax.nn.sigmoid(tok_projected[:, 3 * width_tok :])
    kv_local = tok_projected[:, width_tok : 3 * width_tok].astype(bf16)
    sides = jnp.stack(
        [
            left_side.reshape(devices, part * row_count, tokens),
            right_side.reshape(devices, part * row_count, tokens),
        ],
        axis=1,
    ).reshape(devices, 2 * part * row_count, tokens)
    kv_block = jnp.broadcast_to(
        kv_local.reshape(1, -1, tokens), (devices, kv_local.size // tokens, tokens)
    )
    sent = jnp.concatenate([sides, kv_block], axis=1)
    got = lax.all_to_all(sent, "row", split_axis=0, concat_axis=0, tiled=True)
    sides_all = (
        got[:, : 2 * part * row_count]
        .reshape(devices, 2, part, row_count, tokens)
        .transpose(1, 2, 0, 3, 4)
        .reshape(2, part, tokens, tokens)
    )
    left_cols, right_cols = sides_all[0], sides_all[1]
    kv_all = got[:, 2 * part * row_count :].reshape(tokens, 2 * width_tok)
    crossed = jnp.einsum("cik,cjk->cij", left_cols, right_cols, preferred_element_type=f32).astype(
        bf16
    )
    crossed_rows = lax.all_to_all(crossed, "row", split_axis=1, concat_axis=0, tiled=True)
    crossed_norm = layer_norm(crossed_rows.astype(f32), 0).astype(bf16)
    update = jnp.einsum("cij,cd->ijd", crossed_norm, w_mul_out, preferred_element_type=f32)
    gating = jax.nn.sigmoid(
        jnp.einsum("ijc,cd->ijd", normed, w_mul_gate, preferred_element_type=f32)
    )
    pair_one = (pair_float + gating * update).astype(bf16)
    normed_one = layer_norm(pair_one.astype(f32), -1).astype(bf16)
    projected = jnp.einsum("ijc,cd->ijd", normed_one, w_att_in, preferred_element_type=f32)
    channels = pair_map.shape[2]
    head_tri = w_att_bias.shape[1]
    queries = split_heads(projected[..., :channels].astype(bf16), head_tri)
    keys_in = split_heads(projected[..., channels : 2 * channels].astype(bf16), head_tri)
    values_in = split_heads(projected[..., 2 * channels : 3 * channels].astype(bf16), head_tri)
    gating_att = jax.nn.sigmoid(projected[..., 3 * channels :])
    bias_local = jnp.einsum(
        "ijc,ch->hij", normed_one, w_att_bias, preferred_element_type=f32
    ).astype(bf16)
    tri_scale = (channels // head_tri) ** (-0.5)
    bias_sent = jnp.broadcast_to(bias_local[None], (devices,) + bias_local.shape)
    bias_got = lax.all_to_all(bias_sent, "row", split_axis=0, concat_axis=0, tiled=True)
    bias_all = bias_got.transpose(1, 0, 2, 3).reshape(head_tri, tokens, tokens)

    def attend_row(row_parts):
        return row_attention(
            row_parts[0], row_parts[1], row_parts[2], bias_all, key_shift, tri_scale
        )

    attended = lax.map(attend_row, (queries, keys_in, values_in))
    attended_gated = (gating_att * attended).astype(bf16)
    pair_out = (
        pair_one.astype(f32)
        + jnp.einsum("ijc,cd->ijd", attended_gated, w_att_out, preferred_element_type=f32)
    ).astype(bf16)
    tok_keys = split_heads(kv_all[:, :width_tok], head_tok)
    tok_values = split_heads(kv_all[:, width_tok:], head_tok)
    pair_norm = layer_norm(pair_out.astype(f32), -1).astype(bf16)
    pair_bias = jnp.einsum(
        "ijc,ch->hij", pair_norm, w_pair_bias, preferred_element_type=f32
    ).astype(bf16)
    tok_scale = (width_tok // head_tok) ** (-0.5)
    tok_combined = row_attention(tok_queries, tok_keys, tok_values, pair_bias, key_shift, tok_scale)
    tok_gated = (tok_gate * tok_combined).astype(bf16)
    token_out = (activity + jnp.dot(tok_gated, w_tok_out, preferred_element_type=f32)).astype(bf16)
    return (pair_out, token_out)


def dot_nn(a, b):
    return lax.dot_general(a, b, (((1,), (0,)), ((), ())), preferred_element_type=jnp.float32)


def dot_nt(a, b):
    return lax.dot_general(a, b, (((1,), (1,)), ((), ())), preferred_element_type=jnp.float32)


def lane_norm(values):
    return layer_norm(values, -1).astype(jnp.bfloat16)


def softmax_rows(scores):
    shifted = jnp.exp(scores - jnp.max(scores, axis=-1, keepdims=True))
    return (shifted * (1.0 / jnp.sum(shifted, axis=-1, keepdims=True))).astype(jnp.bfloat16)


def fused_kernel(
    devices,
    *refs,
):
    operands, (pair_out, token_out), refs = refs[:13], refs[13:15], refs[15:]
    held, local_sem, refs = refs[:13], refs[13], refs[14:]
    kernel_body(devices, operands, held, local_sem, pair_out, token_out, *refs)


def kernel_body(
    devices,
    operands,
    held,
    local_sem,
    pair_out,
    token_out,
    send_sides,
    recv_sides,
    send_prod,
    recv_prod,
    send_bias,
    recv_bias,
    send_kv,
    recv_kv,
    wide_sides,
    wide_prod,
    wide_back,
    wide_bias,
    wide_all,
    wide_kv,
    wide_keys,
    wide_w,
    w_sides,
    wide_out,
    send_sem,
    recv_sem,
):
    f32 = jnp.float32
    bf16 = jnp.bfloat16
    me = lax.axis_index("row")
    (
        pair_ref,
        single_ref,
        noise_ref,
        mask_lane,
        w_mul_in,
        w_mul_gate,
        w_mul_out,
        w_att_in,
        w_att_bias,
        w_att_out,
        w_tok_in,
        w_pair_bias,
        w_tok_out,
    ) = held
    loads = [
        pltpu.make_async_copy(source, target, local_sem.at[index])
        for index, (source, target) in enumerate(zip(operands, held))
    ]
    for index in (0, 4, 3, 1, 2, 10, 5, 6, 7, 8, 9, 11, 12):
        loads[index].start()

    barrier = pltpu.get_barrier_semaphore()

    def greet(step, carry):
        other = lax.rem(me + step, devices)
        pl.semaphore_signal(
            barrier, inc=1, device_id={"row": other}, device_id_type=pl.DeviceIdType.MESH
        )
        return carry

    lax.fori_loop(1, devices, greet, 0, unroll=True)

    def send_all(slot, source, landing):
        def one(step, carry):
            other = lax.rem(me + step, devices)
            pltpu.make_async_remote_copy(
                src_ref=source(other),
                dst_ref=landing.at[me],
                send_sem=send_sem.at[slot],
                recv_sem=recv_sem.at[slot],
                device_id={"row": other},
                device_id_type=pl.DeviceIdType.MESH,
            ).start()
            return carry

        lax.fori_loop(1, devices, one, 0, unroll=True)

    def wait_all(sem, landing):
        whole = landing.at[pl.ds(0, devices - 1)]
        pltpu.make_async_copy(whole, whole, sem).wait()

    depth = 4
    plane = devices // depth
    level = lax.div(me, plane)
    seat = lax.rem(me, plane)

    def hop(slot, source, landing, target, other):
        pltpu.make_async_remote_copy(
            src_ref=source,
            dst_ref=landing.at[target],
            send_sem=send_sem.at[slot],
            recv_sem=recv_sem.at[slot],
            device_id={"row": other},
            device_id_type=pl.DeviceIdType.MESH,
        ).start()

    def first_hop(slot, source, landing):
        for step in range(1, depth):
            other = lax.rem(level + step, depth) * plane + seat
            hop(slot, source, landing, seat * depth + level, other)

    def second_hop(slot, landing):
        wait_bytes(recv_sem.at[slot - 1], landing, depth - 1)
        bundle = pl.ds(seat * depth, depth)
        for step in range(1, plane):
            other = level * plane + lax.rem(seat + step, plane)
            hop(slot, landing.at[bundle], landing, bundle, other)

    def wait_bytes(sem, landing, count):
        some = landing.at[pl.ds(0, count)]
        pltpu.make_async_copy(some, some, sem).wait()

    def in_order(landing, wide):
        size = landing.shape[1]
        for position in range(devices):
            start = ((position % depth) * plane + position // depth) * size
            wide[start : start + size, :] = landing[position].astype(f32)

    loads[4].wait()
    wide_w[...] = w_mul_in[...].astype(f32).T
    for kind in range(4):
        for c in range(4):
            w_sides[pl.ds((kind % 2) * 256 + (kind // 2) * 4 + c, devices, stride=8), :] = wide_w[
                pl.ds(kind * 128 + c, devices, stride=4), :
            ]
    loads[0].wait()
    loads[3].wait()
    pair = pair_ref[...].astype(f32)
    normed = lane_norm(pair)
    mixed = dot_nt(w_sides[...].astype(bf16), normed)
    mask = mask_lane[...].astype(f32)
    place = lax.broadcasted_iota(jnp.int32, mask.shape, 1)
    half = w_sides.shape[0] // 2
    blocks = []
    for i in range(4):
        mask_row = jnp.sum(jnp.where(place == me * 4 + i, mask, 0.0), axis=1, keepdims=True)
        cols = slice(i * 128, (i + 1) * 128)
        side = jax.nn.sigmoid(mixed[:half, cols]) * mixed[half:, cols] * (mask * mask_row)
        blocks.append(side.reshape(devices, 8, 128))
    send_sides[...] = jnp.concatenate(blocks, axis=1).astype(bf16)
    recv_sides[me] = send_sides[me]
    pl.semaphore_wait(barrier, devices - 1)
    send_all(0, lambda other: send_sides.at[other], recv_sides)

    for index in (1, 2, 10):
        loads[index].wait()
    activity = single_ref[...].astype(f32) + noise_ref[...].astype(f32)
    activity = jnp.concatenate([activity, jnp.zeros_like(activity)], axis=0)
    tok = dot_nn(lane_norm(activity), w_tok_in[...])
    width = single_ref.shape[1]
    wide_kv[...] = jnp.zeros_like(wide_kv)
    for m in range(6):
        wide_kv[pl.ds(m, 4, stride=8), :] = tok[:4, width + m * 128 : width + (m + 1) * 128]
    send_kv[...] = wide_kv[...].astype(bf16)
    recv_kv[seat * depth + level] = send_kv[...]
    first_hop(2, send_kv, recv_kv)
    for index in (5, 6, 7, 8, 9, 11, 12):
        loads[index].wait()
    gating = jax.nn.sigmoid(dot_nn(normed, w_mul_gate[...]))
    wide_out[...] = w_mul_out[...].astype(f32)
    w_back = jnp.concatenate(
        [wide_out[pl.ds(c, devices, stride=4), :] for c in range(4)], axis=0
    ).astype(bf16)
    w_att_bias_t = jnp.concatenate(
        [w_att_bias[...].astype(f32), jnp.zeros((12, 128), f32)], axis=0
    ).astype(bf16)

    wait_all(recv_sem.at[0], recv_sides)
    wide_sides[...] = recv_sides[...].astype(f32).reshape(wide_sides.shape)
    for c in range(4):
        left = wide_sides[pl.ds(c, 128, stride=8), :].astype(bf16)
        right = wide_sides[pl.ds(4 + c, 128, stride=8), :].astype(bf16)
        wide_prod[pl.ds(c, 128, stride=4), :] = dot_nt(left, right)
    send_prod[...] = wide_prod[...].astype(bf16).reshape(send_prod.shape)
    recv_prod[me] = send_prod[me]
    send_all(1, lambda other: send_prod.at[other], recv_prod)
    wait_all(recv_sem.at[1], recv_prod)
    wide_back[...] = recv_prod[...].astype(f32).reshape(wide_back.shape)
    crossed_norm = []
    for i in range(4):
        crossed = jnp.concatenate(
            [wide_back[pl.ds(i * 4 + c, devices, stride=16), :] for c in range(4)], axis=0
        )
        crossed_norm.append(layer_norm(crossed, 0).T.astype(bf16))
    update = dot_nn(jnp.concatenate(crossed_norm, axis=0), w_back)
    pair_one = (pair + gating * update).astype(bf16).astype(f32)

    normed_one = lane_norm(pair_one)
    bias = dot_nt(w_att_bias_t, normed_one)
    for i in range(4):
        wide_bias[i * 4 : (i + 1) * 4, :] = bias[:4, i * 128 : (i + 1) * 128]
    send_bias[...] = wide_bias[...].astype(bf16)
    recv_bias[me] = send_bias[...]
    send_all(4, lambda other: send_bias, recv_bias)
    second_hop(3, recv_kv)
    projected = dot_nn(normed_one, w_att_in[...])
    shift = jnp.where(mask > 0, 0.0, -1000000000.0).astype(f32)
    head_of = lax.broadcasted_iota(jnp.int32, (128, 128), 1) // 32
    raw = []
    for i in range(4):
        rows = slice(i * 128, (i + 1) * 128)
        query = projected[rows, :128]
        query = jnp.concatenate([jnp.where(head_of == h, query, 0.0) for h in range(4)], axis=0)
        raw.append(dot_nt(query.astype(bf16), projected[rows, 128:256].astype(bf16)))

    wait_all(recv_sem.at[4], recv_bias)
    wide_all[...] = recv_bias[...].astype(f32).reshape(wide_all.shape)
    bias_all = jnp.concatenate(
        [wide_all[pl.ds(h, 128, stride=4), :] for h in range(4)], axis=0
    )
    scale = 32.0**-0.5
    gated = []
    for i in range(4):
        rows = slice(i * 128, (i + 1) * 128)
        weights = softmax_rows(raw[i] * scale + bias_all + shift)
        spread = dot_nn(weights, projected[rows, 256:384].astype(bf16))
        attended = jnp.zeros((128, 128), f32)
        for h in range(4):
            attended = jnp.where(head_of == h, spread[h * 128 : (h + 1) * 128], attended)
        gated.append((jax.nn.sigmoid(projected[rows, 384:]) * attended).astype(bf16))
    final = (pair_one + dot_nn(jnp.concatenate(gated, axis=0), w_att_out[...])).astype(bf16)
    pair_out[...] = final

    pair_bias = dot_nt(w_pair_bias[...], lane_norm(final.astype(f32))).astype(bf16).astype(f32)
    pair_bias = jnp.concatenate([pair_bias[:, i * 128 : (i + 1) * 128] for i in range(4)], axis=0)
    lane = lax.broadcasted_iota(jnp.int32, (16, width), 1)
    head = lax.broadcasted_iota(jnp.int32, (16, width), 0)
    own = (lane >= head * 24) & (lane < head * 24 + 24)
    query = jnp.concatenate([jnp.where(own, tok[i : i + 1, :width], 0.0) for i in range(4)], axis=0)
    wait_bytes(recv_sem.at[3], recv_kv, devices - depth)
    in_order(recv_kv, wide_keys)
    chunks = [wide_keys[pl.ds(m, 128, stride=8), :].astype(bf16) for m in range(6)]
    keys = jnp.concatenate(chunks[:3], axis=1)
    values = jnp.concatenate(chunks[3:], axis=1)
    weights = softmax_rows(dot_nt(query.astype(bf16), keys) * 24.0**-0.5 + pair_bias + shift)
    spread = dot_nn(weights, values)
    combined = jnp.concatenate(
        [
            jnp.sum(jnp.where(own, spread[i * 16 : (i + 1) * 16], 0.0), axis=0, keepdims=True)
            for i in range(4)
        ]
        + [jnp.zeros((4, width), f32)],
        axis=0,
    )
    tok_gated = (jax.nn.sigmoid(tok[:, 3 * width :]) * combined).astype(bf16)
    token_out[...] = (activity + dot_nn(tok_gated, w_tok_out[...]))[:4].astype(bf16)

    wait_all(send_sem.at[0], recv_sides)
    wait_all(send_sem.at[1], recv_prod)
    wait_all(send_sem.at[4], recv_bias)
    wait_bytes(send_sem.at[2], recv_kv, depth - 1)
    wait_bytes(send_sem.at[3], recv_kv, devices - depth)


def fused(
    pair_map,
    single,
    noise_term,
    token_mask,
    w_mul_in,
    w_mul_gate,
    w_mul_out,
    w_att_in,
    w_att_bias,
    w_att_out,
    w_tok_in,
    w_pair_bias,
    w_tok_out,
):
    bf16 = jnp.bfloat16
    f32 = jnp.float32
    devices = lax.axis_size("row")
    operands = (
        pair_map.reshape(512, 128),
        single,
        noise_term,
        token_mask.reshape(1, -1),
        w_mul_in,
        w_mul_gate,
        w_mul_out,
        w_att_in,
        w_att_bias.T,
        w_att_out,
        w_tok_in,
        w_pair_bias.T,
        w_tok_out,
    )
    vmem = pl.BlockSpec(memory_space=pltpu.VMEM)
    pair_out, token_out = pl.pallas_call(
        functools.partial(fused_kernel, devices),
        out_shape=(
            jax.ShapeDtypeStruct((512, 128), bf16),
            jax.ShapeDtypeStruct(single.shape, bf16),
        ),
        in_specs=[pl.BlockSpec(memory_space=pl.ANY)] * 13,
        out_specs=(vmem, vmem),
        scratch_shapes=[pltpu.VMEM(held.shape, held.dtype) for held in operands]
        + [
            pltpu.SemaphoreType.DMA((13,)),
            pltpu.VMEM((devices, 32, 128), bf16),
            pltpu.VMEM((devices, 32, 128), bf16),
            pltpu.VMEM((devices, 16, 128), bf16),
            pltpu.VMEM((devices, 16, 128), bf16),
            pltpu.VMEM((16, 128), bf16),
            pltpu.VMEM((devices, 16, 128), bf16),
            pltpu.VMEM((32, 128), bf16),
            pltpu.VMEM((devices, 32, 128), bf16),
            pltpu.VMEM((devices * 32, 128), f32),
            pltpu.VMEM((devices * 16, 128), f32),
            pltpu.VMEM((devices * 16, 128), f32),
            pltpu.VMEM((16, 128), f32),
            pltpu.VMEM((devices * 16, 128), f32),
            pltpu.VMEM((32, 128), f32),
            pltpu.VMEM((devices * 32, 128), f32),
            pltpu.VMEM((512, 128), f32),
            pltpu.VMEM((512, 128), f32),
            pltpu.VMEM((128, 128), f32),
            pltpu.SemaphoreType.DMA((6,)),
            pltpu.SemaphoreType.DMA((6,)),
        ],
        compiler_params=pltpu.CompilerParams(
            collective_id=0, has_side_effects=True, vmem_limit_bytes=56 * 1024 * 1024
        ),
    )(*operands)
    return pair_out.reshape(pair_map.shape), token_out


def solution(mesh):
    placed = (
        P(("grp", "row"), None, None),
        P(("grp", "row"), None),
        P(("grp", "row"), None),
        P("grp"),
        P(),
        P(),
        P(),
        P(),
        P(),
        P(),
        P(),
        P(),
        P(),
    )

    def body(*arrays):
        devices = mesh.shape["row"]
        fits = arrays[0].shape == (4, 128, 128) and devices == 32
        fits = fits and arrays[1].shape[1] == 384 and arrays[4].shape[1] == 512
        return fused(*arrays) if fits else per_device(*arrays)

    return jax.shard_map(
        body,
        mesh=mesh,
        in_specs=placed,
        out_specs=(P(("grp", "row"), None, None), P(("grp", "row"), None)),
        check_vma=False,
    )
```
